256 devices in a mesh: rep: 8 (over x, core), exp: 32 (over y, z).
Axes of the slice: x: 4, y: 4, z: 8, core: 2. Of those that a mesh axis runs over, the one named last changes fastest.
Arguments:
- latent: float32 [32768, 2048], P(('rep', 'exp')), may hold values from -6 to 6
- targets: bfloat16 [1, 32768, 2048], P(None, ('rep', 'exp')), may hold values from -6 to 6
- norm_gain: float32 [2048], replicated, may hold values from 0.25 to 1.75
- router: bfloat16 [2048, 32], replicated, may hold values from -0.125 to 0.125
- expert_ids: int32 [1, 32768, 6], P(None, ('rep', 'exp')), may hold values from 0 to 31, all different within a row; in each aligned block of 128 rows (0 to 127, 128 to 255, ..., all dimensions but the last counted through in order) at most 25 rows name the same one
- gate_valid: int32 [1, 32768, 6], P(None, ('rep', 'exp')), may hold values 0 or 1
- w_gate: bfloat16 [32, 2048, 704], P('exp', 'rep'), may hold values from -0.125 to 0.125
- w_up: bfloat16 [32, 2048, 704], P('exp', 'rep'), may hold values from -0.125 to 0.125
- w_down: bfloat16 [32, 704, 2048], P('exp', None, 'rep'), may hold values from -0.21875 to 0.21875
Outputs:
- grad_latent: float32 [32768, 2048], P(('rep', 'exp'))
- grad_router: float32 [2048, 32], replicated
- grad_gain: float32 [2048], replicated
The draws below stay inside these ranges and needn't reach their ends.
Inputs may be any that keep to these rules, and one draw needn't show every extreme that they name: `expert_ids`: within the 128 tokens of one device at one step, the 6 picks of a token differ, no expert is named more than 25 times, a bound that some block reaches.
All inputs are finite; a program needn't handle non-finite values. No bound on the sum of `gate_valid` on one device may be relied on, other than what follows from the above.
Results may differ from the reference program's by a relative error of at most 0.0051.
Values may be sent and summed in bfloat16 or wider, within the bound.
No kernel may reach another device: no remote copies, remote signals or barrier semaphores. Data moves between devices by JAX's collectives and lax.ppermute only.
A program may use at most 128 MiB of HBM per device.

```python
import math
import jax
import jax.numpy as jnp
import numpy as np
from jax import lax

D = 2048
FF = 704
TOPK = 6
UNROLL = 1
TOK_DEV = 128
EXPERTS = 32
CAP = 25
TOKENS = 32768
N_REP = 8
N_EXP = 32


def set_ends(values, stream_key, smallest, largest):
    longest = values.shape.index(max(values.shape))
    spots = []
    for shift in (0, 1):
        where = [jax.random.randint(jax.random.fold_in(stream_key, axis), (), 0, length) for axis, length in enumerate(values.shape)]
        where[longest] = (where[longest] + shift) % values.shape[longest]
        spots.append(tuple(where))
    return values.at[spots[0]].set(smallest).at[spots[1]].set(largest)


def level_of(rng, dims, pieces, smallest, top_value):
    def one(axis_at, shards_of):
        heights = jax.random.uniform(jax.random.fold_in(jax.random.fold_in(rng, 6), axis_at), (shards_of,), jnp.float32, smallest / len(pieces), top_value / len(pieces))
        return jnp.repeat(jnp.exp(heights), dims[axis_at] // shards_of).reshape((-1,) + (1,) * (len(dims) - axis_at - 1))

    gain = one(*pieces[0])
    for cut in pieces[1:]:
        gain = gain * one(*cut)
    return gain


def shared_out(stream_key, own, number, rows, amount, top, reach, lean):
    order = jax.random.permutation(stream_key, amount)
    crowded, common = load_shares(amount, rows * top, reach, lean, True), load_shares(amount, rows * top, reach, lean, False)
    places = jnp.arange(amount)

    def named(lengths, turn):
        used = int((lengths > 0).sum())
        fixed = max(1, used // 4)
        shifted = fixed + (places - fixed + turn * (used - fixed)) % max(1, amount - fixed)
        return jnp.zeros((amount,), jnp.int32).at[order[jnp.where(places < fixed, places, shifted)]].set(jnp.asarray(lengths, jnp.int32))

    lengths = jnp.where(number % 4 == 0, named(crowded, number // 4), named(common, number - number // 4 - 1))
    mixed = jax.random.permutation(jax.random.fold_in(own, 3), amount)
    donor, receiver = mixed[0:amount // 2 * 2:2], mixed[1:amount // 2 * 2:2]
    room = jnp.minimum(lengths[donor] - 1, reach - lengths[receiver]) // 2
    room = jnp.where((donor == order[0]) | (receiver == order[0]) | (lengths[receiver] == 0), 0, jnp.maximum(room, 0))
    shifted = jax.random.randint(jax.random.fold_in(own, 4), (amount // 2,), 0, 1 << 20) % (room + 1)
    lengths = lengths.at[donor].add(-shifted).at[receiver].add(shifted)
    members = jnp.searchsorted(jnp.cumsum(lengths), jnp.arange(rows * top), side="right").astype(jnp.int32)
    grid = members.reshape(top, rows).T
    grid = grid[jax.random.permutation(jax.random.fold_in(own, 1), rows)]
    turn = jax.random.randint(jax.random.fold_in(own, 2), (rows, 1), 0, top)
    return jnp.take_along_axis(grid, (jnp.arange(top)[None, :] + turn) % top, axis=1)


def load_shares(count, total, bound, slope, full):
    weights = [(1 << 20) // math.isqrt(rank ** slope) + 1 for rank in range(1, count + 1)]
    largest = bound if full else min(bound, max(-(-total // count), total * weights[0] // sum(weights)))
    least = 1 if total - largest >= count - 1 else 0
    holding, rest = [largest] + [least] * (count - 1), total - largest - least * (count - 1)
    while rest > 0:
        movable = [i for i in range(1, count) if holding[i] < largest] or [i for i in range(1, count) if holding[i] < bound]
        mass, budget = sum([weights[i] for i in movable]), rest
        for i in movable:
            addition = min(bound - holding[i], max(1, budget * weights[i] // mass), rest)
            holding[i] = holding[i] + addition
            rest = rest - addition
    return np.array(holding)


def centred(key, extent, spread, reach, split=(), held_as=jnp.bfloat16):
    gain = level_of(key, extent, split, -0.22, 0.18) if split else 1.0
    entries = jax.random.normal(key, extent, jnp.float32) * spread * gain
    return jnp.minimum(jnp.maximum(entries, -reach), reach).astype(held_as)


def setup_inputs(seed: int = 0) -> dict:
    splits = jax.random.split(jax.random.key(seed), 10)
    latent = centred(splits[0], (TOKENS, D), 1.0, 6.0, ((0, 256),), jnp.float32)
    targets = centred(splits[1], (UNROLL, TOKENS, D), 1.0, 6.0, ((1, 256),))
    norm_gain = jnp.clip(1.0 + 0.15 * jax.random.normal(splits[2], (D,), jnp.float32), 0.25, 1.75)
    router = centred(splits[3], (D, EXPERTS), D ** -0.5, 0.125)
    expert_ids_keys = jax.random.split(jax.random.fold_in(splits[4], 1), UNROLL * TOKENS // TOK_DEV)
    expert_ids_turns = jax.random.permutation(jax.random.fold_in(splits[4], 3), UNROLL * TOKENS // TOK_DEV)
    expert_ids = jax.vmap(lambda own, number: shared_out(jax.random.fold_in(splits[4], 2), own, number, TOK_DEV, EXPERTS, TOPK, CAP, 2))(expert_ids_keys, expert_ids_turns).reshape((UNROLL, TOKENS, TOPK))
    gate_valid = set_ends((jax.random.randint(splits[5], (UNROLL, TOKENS, TOPK), 0, 8) < 7).astype(jnp.int32), jax.random.fold_in(splits[5], 1), 0, 1)
    w_gate = centred(splits[6], (EXPERTS, D, FF), D ** -0.5, 0.125, ((0, 32), (1, 8)))
    w_up = centred(splits[7], (EXPERTS, D, FF), D ** -0.5, 0.125, ((0, 32), (1, 8)))
    w_down = centred(splits[8], (EXPERTS, FF, D), FF ** -0.5, 0.21875, ((0, 32), (2, 8)))
    return dict(latent=latent, targets=targets, norm_gain=norm_gain, router=router, expert_ids=expert_ids, gate_valid=gate_valid, w_gate=w_gate, w_up=w_up, w_down=w_down)


epsilon = 1e-06

def norm_rows(latent, norm_gain):
    inv_scale = lax.rsqrt(lax.optimization_barrier(jnp.mean(latent * latent, axis=-1, keepdims=True)) + epsilon)
    return (inv_scale, (latent * inv_scale * norm_gain).astype(jnp.bfloat16))

def positions(chosen_ids):
    total_rows, top_count = chosen_ids.shape
    blocks = total_rows // TOK_DEV
    flat_ids = chosen_ids.reshape(blocks, TOK_DEV * top_count)
    onehot = (flat_ids[:, :, None] == jnp.arange(EXPERTS, dtype=jnp.int32)[None, None, :]).astype(jnp.int32)
    before = jnp.cumsum(onehot, axis=1) - onehot
    slot_index = lax.optimization_barrier(jnp.sum(before * onehot, axis=2))
    anchor = jnp.arange(blocks, dtype=jnp.int32)[:, None] * CAP
    return (anchor + slot_index).reshape(total_rows, top_count).astype(jnp.int32)

def to_buffers(values, chosen_ids, placing):
    row_limit = N_EXP * CAP
    flat_values = values.reshape(-1, values.shape[-1])

    def one_expert(expert):
        target_rows = jnp.where(chosen_ids == expert, placing, row_limit).reshape(-1)
        empty = jnp.zeros((row_limit, values.shape[-1]), values.dtype)
        return empty.at[target_rows].set(flat_values, mode='drop')
    return lax.map(one_expert, jnp.arange(EXPERTS, dtype=jnp.int32))

def expert_forward(inputs):
    row_block, gate_weight, up_weight, down_weight = inputs
    hidden_gate = jnp.dot(row_block, gate_weight, preferred_element_type=jnp.float32)
    hidden_up = jnp.dot(row_block, up_weight, preferred_element_type=jnp.float32)
    activated = (jax.nn.silu(hidden_gate) * hidden_up).astype(jnp.bfloat16)
    expert_out = jnp.dot(activated, down_weight, preferred_element_type=jnp.float32).astype(jnp.bfloat16)
    return (expert_out, hidden_gate, hidden_up)

def expert_backward(inputs):
    grad_in, hidden_gate, hidden_up, gate_weight, up_weight, down_weight = inputs
    grad_act = jnp.dot(grad_in, down_weight.T, preferred_element_type=jnp.float32).astype(jnp.bfloat16)
    sigmoid_gate = jax.nn.sigmoid(hidden_gate)
    act_grad = grad_act.astype(jnp.float32)
    grad_hidden_gate = (act_grad * hidden_up * sigmoid_gate * (1.0 + hidden_gate * (1.0 - sigmoid_gate))).astype(jnp.bfloat16)
    grad_hidden_up = (act_grad * jax.nn.silu(hidden_gate)).astype(jnp.bfloat16)
    grad_rows = (jnp.dot(grad_hidden_gate, gate_weight.T, preferred_element_type=jnp.float32) + jnp.dot(grad_hidden_up, up_weight.T, preferred_element_type=jnp.float32)).astype(jnp.bfloat16)
    return grad_rows

def rep_group(latent, targets, expert_ids, gate_valid, norm_gain, router, w_gate, w_up, w_down):
    experts_row = jnp.arange(EXPERTS, dtype=jnp.int32)
    latent_now = latent
    saved = []
    for unroll in range(UNROLL):
        chosen_ids = expert_ids[unroll]
        validity = gate_valid[unroll].astype(jnp.float32)
        inv_scale, normed = norm_rows(latent_now, norm_gain)
        logits = jnp.dot(normed, router, preferred_element_type=jnp.float32)
        sigmoid_pick = jax.nn.sigmoid(jnp.take_along_axis(logits, chosen_ids, axis=1))
        gating = sigmoid_pick * validity
        placing = positions(chosen_ids)
        spread_rows = jnp.broadcast_to(normed[:, None, :], chosen_ids.shape + (D,))
        row_blocks = to_buffers(spread_rows, chosen_ids, placing)
        expert_out, hidden_gate, hidden_up = lax.map(expert_forward, (row_blocks, w_gate, w_up, w_down))
        picked_out = expert_out[chosen_ids, placing].astype(jnp.float32)
        mixed = lax.optimization_barrier(jnp.sum(gating[:, :, None] * picked_out, axis=1))
        saved.append((latent_now, inv_scale, normed, sigmoid_pick, validity, gating, placing, hidden_gate, hidden_up, picked_out))
        latent_now = latent_now + mixed
    cotangent = latent_now - targets[UNROLL - 1].astype(jnp.float32)
    router_grad = jnp.zeros((D, EXPERTS), jnp.float32)
    gain_grad = jnp.zeros((D,), jnp.float32)
    for unroll in reversed(range(UNROLL)):
        earlier, inv_scale, normed, sigmoid_pick, validity, gating, placing, hidden_gate, hidden_up, picked_out = saved[unroll]
        chosen_ids = expert_ids[unroll]
        grad_gating = lax.optimization_barrier(jnp.sum(cotangent[:, None, :] * picked_out, axis=2))
        grad_out = (gating[:, :, None] * cotangent[:, None, :]).astype(jnp.bfloat16)
        grad_blocks = to_buffers(grad_out, chosen_ids, placing)
        grad_rows = lax.map(expert_backward, (grad_blocks, hidden_gate, hidden_up, w_gate, w_up, w_down))
        grad_normed = lax.optimization_barrier(jnp.sum(grad_rows[chosen_ids, placing].astype(jnp.float32), axis=1))
        grad_pick = grad_gating * validity * sigmoid_pick * (1.0 - sigmoid_pick)
        onehot = (chosen_ids[:, :, None] == experts_row[None, None, :]).astype(jnp.float32)
        grad_logits = lax.optimization_barrier(jnp.sum(grad_pick[:, :, None] * onehot, axis=1)).astype(jnp.bfloat16)
        router_grad = router_grad + jnp.dot(normed.T, grad_logits, preferred_element_type=jnp.float32)
        grad_normed = grad_normed + jnp.dot(grad_logits, router.T, preferred_element_type=jnp.float32)
        gain_grad = gain_grad + lax.optimization_barrier(jnp.sum(grad_normed * earlier * inv_scale, axis=0))
        scaled = grad_normed * norm_gain
        cube = inv_scale * inv_scale * inv_scale
        cotangent = cotangent + inv_scale * scaled - earlier * cube * lax.optimization_barrier(jnp.mean(scaled * earlier, axis=-1, keepdims=True))
        if unroll > 0:
            cotangent = cotangent + (earlier - targets[unroll - 1].astype(jnp.float32))
    return (cotangent, router_grad, gain_grad)

def reference(latent, targets, norm_gain, router, expert_ids, gate_valid, w_gate, w_up, w_down):
    group_rows = N_EXP * TOK_DEV
    latents = latent.reshape(N_REP, group_rows, D)
    goal_rows = targets.reshape(UNROLL, N_REP, group_rows, D).transpose(1, 0, 2, 3)
    routes = expert_ids.reshape(UNROLL, N_REP, group_rows, TOPK).transpose(1, 0, 2, 3)
    mask_rows = gate_valid.reshape(UNROLL, N_REP, group_rows, TOPK).transpose(1, 0, 2, 3)

    def scan_group(carry, inputs):
        group_latent, group_goal, group_route, group_mask = inputs
        result = rep_group(group_latent, group_goal, group_route, group_mask, norm_gain, router, w_gate, w_up, w_down)
        return ((carry[0] + result[1], carry[1] + result[2]), result[0])
    start = (jnp.zeros((D, EXPERTS), jnp.float32), jnp.zeros((D,), jnp.float32))
    totals, grad_rows = lax.scan(scan_group, start, (latents, goal_rows, routes, mask_rows))
    return (grad_rows.reshape(TOKENS, D), totals[0], totals[1])
```

```python
import jax
import jax.numpy as jnp
from jax import lax
from jax.experimental import pallas as pl
from jax.experimental.pallas import tpu as pltpu
from jax.sharding import Mesh, PartitionSpec as P

N_X, N_C, N_Y, N_Z = 4, 2, 4, 8
TOP = 6
LOCAL = 128
COLUMN = N_Z * LOCAL
CAP = 25
ROWS = 208
D = 2048
FF = 704
N_REP = N_X * N_C
SHARD = D // N_REP
EPS = 1e-06
F32, BF16 = jnp.float32, jnp.bfloat16
UP = [(i, (i + 1) % N_Z) for i in range(N_Z)]
DOWN = [(i, (i - 1) % N_Z) for i in range(N_Z)]


def dot(left, right):
    return jnp.dot(left, right, preferred_element_type=F32)


def dot_last(left, right):
    return lax.dot_general(left, right, (((1,), (1,)), ((), ())), preferred_element_type=F32)


def forward_kernel(x_ref, w_ref, gate_ref, spread_ref, eo_ref, hg_ref, hu_ref, out_ref, rows_ref):
    j = pl.program_id(0)
    hg = jnp.zeros((ROWS, FF), F32)
    hu = jnp.zeros((ROWS, FF), F32)
    for r in range(N_REP):
        x = x_ref[0, :, r * SHARD : (r + 1) * SHARD]
        hg += dot_last(x, w_ref[0, r, :, 0:SHARD])
        hu += dot_last(x, w_ref[0, r, :, SHARD : 2 * SHARD])
    hg_ref[0] = hg
    hu_ref[0] = hu
    act = (hg * jax.nn.sigmoid(hg) * hu).astype(BF16)
    gate = gate_ref[0]
    start = pl.multiple_of(j * ROWS, 16)
    for r in range(N_REP):
        cols = slice(r * SHARD, (r + 1) * SHARD)
        eo = dot(act, w_ref[0, r, :, 2 * SHARD : 3 * SHARD]).astype(BF16)
        eo_ref[0, :, cols] = eo
        rows_ref[pl.ds(start, ROWS), cols] = (eo.astype(F32) * gate).astype(BF16)

    @pl.when(j == N_Y - 1)
    def _():
        for r in range(N_REP):
            cols = slice(r * SHARD, (r + 1) * SHARD)
            out_ref[:, cols] = dot(spread_ref[...], rows_ref[:, cols]).astype(BF16)


def backward_kernel(
    c_ref, p_ref, x_ref, w_ref, gate_ref, slope_ref, eo_ref, hg_ref, hu_ref, router_ref, gain_ref, spread_ref,
    out_ref, router_grad_ref, gain_grad_ref, rows_ref,
):
    j = pl.program_id(0)
    gate = gate_ref[0]
    pick = p_ref[0]
    grad_act = jnp.zeros((ROWS, FF), F32)
    grad_gating = jnp.zeros((ROWS, 1), F32)
    for r in range(N_REP):
        cols = slice(r * SHARD, (r + 1) * SHARD)
        c = dot(pick, c_ref[:, cols])
        grad_gating += jnp.sum(c * eo_ref[0, :, cols].astype(F32), axis=1, keepdims=True)
        grad_act += dot_last((gate * c).astype(BF16), w_ref[0, r, :, 2 * SHARD : 3 * SHARD])
    grad_act = grad_act.astype(BF16).astype(F32)
    hg = hg_ref[0]
    s = jax.nn.sigmoid(hg)
    grad_hg = (grad_act * hu_ref[0] * s * (1.0 + hg * (1.0 - s))).astype(BF16)
    grad_hu = (grad_act * (hg * s)).astype(BF16)
    grad_logit = (grad_gating * slope_ref[0]).astype(BF16).astype(F32)
    start = pl.multiple_of(j * ROWS, 16)

    @pl.when(j == 0)
    def _():
        gain_grad_ref[...] = jnp.zeros_like(gain_grad_ref)

    for r in range(N_REP):
        cols = slice(r * SHARD, (r + 1) * SHARD)
        rows = dot(grad_hg, w_ref[0, r, :, 0:SHARD]) + dot(grad_hu, w_ref[0, r, :, SHARD : 2 * SHARD])
        rows = rows.astype(BF16).astype(F32) + grad_logit * router_ref[0, :, cols]
        x = x_ref[0, :, cols].astype(F32)
        router_grad_ref[0, :, cols] = jnp.sum(x * grad_logit, axis=0, keepdims=True)
        gain_grad_ref[:, cols] += jnp.sum(x * rows, axis=0, keepdims=True)
        rows_ref[pl.ds(start, ROWS), cols] = rows.astype(BF16)

    @pl.when(j == N_Y - 1)
    def _():
        gain_grad_ref[...] = gain_grad_ref[...] / gain_ref[...]
        for r in range(N_REP):
            cols = slice(r * SHARD, (r + 1) * SHARD)
            out_ref[:, cols] = dot(spread_ref[...], rows_ref[:, cols]).astype(BF16)


def whole(*shape):
    return pl.BlockSpec(shape, lambda j: (0,) * len(shape))


def each(*shape):
    return pl.BlockSpec((1,) + shape, lambda j: (j,) + (0,) * len(shape))


PARAMS = pltpu.CompilerParams(dimension_semantics=("arbitrary",), vmem_limit_bytes=60 * 1024 * 1024)


def expert_forward(x, weights, gate, spread):
    shape = jax.ShapeDtypeStruct
    return pl.pallas_call(
        forward_kernel,
        grid=(N_Y,),
        in_specs=[each(ROWS, D), each(N_REP, FF, 3 * SHARD), each(ROWS, 1), whole(COLUMN, N_Y * ROWS)],
        out_specs=[each(ROWS, D), each(ROWS, FF), each(ROWS, FF), whole(COLUMN, D)],
        out_shape=[
            shape((N_Y, ROWS, D), BF16),
            shape((N_Y, ROWS, FF), F32),
            shape((N_Y, ROWS, FF), F32),
            shape((COLUMN, D), BF16),
        ],
        scratch_shapes=[pltpu.VMEM((N_Y * ROWS, D), BF16)],
        compiler_params=PARAMS,
        name="expert_forward",
    )(x, weights, gate, spread)


def expert_backward(c, pick, x, weights, gate, slope, eo, hg, hu, router, gain, spread):
    shape = jax.ShapeDtypeStruct
    return pl.pallas_call(
        backward_kernel,
        grid=(N_Y,),
        in_specs=[
            whole(COLUMN, D), each(ROWS, COLUMN), each(ROWS, D), each(N_REP, FF, 3 * SHARD), each(ROWS, 1), each(ROWS, 1),
            each(ROWS, D), each(ROWS, FF), each(ROWS, FF), each(1, D), whole(1, D), whole(COLUMN, N_Y * ROWS),
        ],
        out_specs=[whole(COLUMN, D), each(1, D), whole(1, D)],
        out_shape=[shape((COLUMN, D), BF16), shape((N_Y, 1, D), F32), shape((1, D), F32)],
        scratch_shapes=[pltpu.VMEM((N_Y * ROWS, D), BF16)],
        compiler_params=PARAMS,
        name="expert_backward",
    )(c, pick, x, weights, gate, slope, eo, hg, hu, router, gain, spread)


def ring_gather(block, chains):
    width = block.shape[1] // chains
    parts = []
    for i in range(chains):
        up = [block[:, i * width : (i + 1) * width]]
        down = [up[0]]
        parts.append((up, down))
    for step in range(4):
        for up, down in parts:
            up.append(lax.ppermute(up[-1], "z", UP))
            if step < 3:
                down.append(lax.ppermute(down[-1], "z", DOWN))
    return [parts[i][0] + parts[i][1][:0:-1] for i in range(chains)]


def in_order(blocks, z):
    stacked = jnp.stack([jnp.concatenate(b, axis=1) for b in zip(*blocks)])
    backwards = jnp.stack([stacked[(-k) % N_Z] for k in range(N_Z)])
    return jnp.roll(backwards, z, axis=0)


def shards(latent, targets, norm_gain, router, expert_ids, gate_valid, w_gate, w_up, w_down):
    y_axes = ("y", "x", "c")
    z = lax.axis_index("z")
    own = jnp.concatenate([w_gate[0].T, w_up[0].T, w_down[0]], axis=1)
    weights = lax.all_gather(own, y_axes, axis=0, tiled=False).reshape(N_Y, N_REP, FF, 3 * SHARD)

    inv_scale = lax.rsqrt(jnp.mean(latent * latent, axis=-1, keepdims=True) + EPS)
    normed = (latent * inv_scale * norm_gain).astype(BF16)
    codes = (expert_ids[0] + 32 * gate_valid[0]).T
    codes = jnp.concatenate([codes, jnp.zeros((2, LOCAL), jnp.int32)], axis=0)

    column = jnp.concatenate([jnp.concatenate(b, axis=1) for b in zip(*ring_gather(normed, 2))], axis=0)
    column_codes = jnp.concatenate(ring_gather(codes, 1)[0], axis=1)[:TOP]
    ids, valid = column_codes % 32, column_codes // 32

    mine = jnp.arange(N_Y, dtype=jnp.int32) * N_Z + z
    hit = ids[None] == mine[:, None, None]
    chosen = jnp.any(hit, axis=1)
    valid_here = jnp.sum(jnp.where(hit, valid[None], 0), axis=1).astype(F32)
    token = jnp.arange(COLUMN, dtype=jnp.int32)
    earlier = (token[:, None] < token[None, :]).astype(BF16)
    rank = dot(chosen.astype(BF16), earlier).astype(jnp.int32)
    rank = jnp.where(chosen, rank, -1)
    slot = jnp.arange(ROWS, dtype=jnp.int32)
    at = rank[:, None, :] == slot[None, :, None]
    x = dot(at.astype(BF16).reshape(N_Y * ROWS, COLUMN), column).astype(BF16).reshape(N_Y, ROWS, D)
    rank = by_owner(rank, z)
    pick = (rank[:, None, :] == slot[None, :, None]).astype(BF16)
    spread = (
        (rank.T[:, :, None] == slot[None, None, :]).astype(BF16).reshape(COLUMN, N_Y * ROWS)
    )
    router_here = lax.dynamic_index_in_dim(router.reshape(D, N_Y, N_Z), z, 2, keepdims=False).T.astype(F32)
    logit = jnp.sum(x.astype(F32) * router_here[:, None, :], axis=2)
    sigmoid_pick = jax.nn.sigmoid(logit)
    valid_row = jnp.sum(jnp.where(at, valid_here[:, None, :], 0.0), axis=2)
    gate = (sigmoid_pick * valid_row)[:, :, None]
    slope = (valid_row * sigmoid_pick * (1.0 - sigmoid_pick))[:, :, None]

    eo, hg, hu, mixed = expert_forward(x, weights, gate, spread)
    mixed = scatter_sum(mixed)
    cotangent = latent + mixed.astype(F32) - targets[0].astype(F32)
    c = gather_column(cotangent.astype(BF16))
    back, router_grad, gain_grad = expert_backward(
        c, pick, x, weights, gate, slope, eo, hg, hu, router_here[:, None, :], norm_gain[None], spread
    )
    grad_normed = scatter_sum(back).astype(F32)

    sums = jnp.concatenate([router_grad[:, 0], gain_grad, jnp.zeros((3, D), F32)], axis=0)
    sums = sums + lax.ppermute(sums, "c", [(0, 1), (1, 0)])
    for axis in ("x", "y"):
        for flip in (1, 2):
            sums = sums + lax.ppermute(sums, axis, [(i, i ^ flip) for i in range(4)])
    sums = in_order(ring_gather(sums, 1), z)
    grad_router = sums[:, :N_Y].transpose(2, 1, 0).reshape(D, N_Y * N_Z)
    grad_gain = jnp.sum(sums[:, N_Y], axis=0)

    scaled = grad_normed * norm_gain
    cube = inv_scale * inv_scale * inv_scale
    grad_latent = (
        cotangent + inv_scale * scaled - latent * cube * jnp.mean(scaled * latent, axis=-1, keepdims=True)
    )
    return grad_latent, grad_router, grad_gain


def by_owner(values, z):
    blocks = values.reshape(-1, N_Z, LOCAL)
    return jnp.stack([lax.dynamic_index_in_dim(blocks, (z - k) % N_Z, 1, keepdims=False) for k in range(N_Z)], axis=1).reshape(
        -1, COLUMN
    )


def scatter_sum(partial):
    return lax.psum_scatter(partial, "z", scatter_dimension=0, tiled=True)


def gather_column(block):
    return lax.all_gather(block, "z", axis=0, tiled=True)


def solution(mesh):
    split = Mesh(mesh.devices.reshape(N_X, N_C, N_Y, N_Z), ("x", "c", "y", "z"))
    every = ("x", "c", "y", "z")
    rep, exp = ("x", "c"), ("y", "z")
    return jax.shard_map(
        shards,
        mesh=split,
        in_specs=(
            P(every, None),
            P(None, every, None),
            P(),
            P(),
            P(None, every, None),
            P(None, every, None),
            P(exp, rep, None),
            P(exp, rep, None),
            P(exp, None, rep),
        ),
        out_specs=(P(every, None), P(), P()),
        check_vma=False,
    )
```

```python
import jax
import jax.numpy as jnp
from jax import lax
from jax.experimental import pallas as pl
from jax.experimental.pallas import tpu as pltpu
from jax.sharding import Mesh, PartitionSpec as P

N_X, N_C, N_Y, N_Z = 4, 2, 4, 8
TOP = 6
LOCAL = 128
COLUMN = N_Z * LOCAL
CAP = 25
ROWS = 208
D = 2048
FF = 704
N_REP = N_X * N_C
SHARD = D // N_REP
PART = 6
EPS = 1e-06
F32, BF16 = jnp.float32, jnp.bfloat16
UP = [(i, (i + 1) % N_Z) for i in range(N_Z)]
DOWN = [(i, (i - 1) % N_Z) for i in range(N_Z)]


def dot(left, right):
    return jnp.dot(left, right, preferred_element_type=F32)


def dot_last(left, right):
    return lax.dot_general(left, right, (((1,), (1,)), ((), ())), preferred_element_type=F32)


def forward_kernel(
    x_ref, w_ref, gate_ref, spread_ref, spread_near_ref, eo_ref, hg_ref, hu_ref, out_ref, near_ref, rows_ref
):
    j = pl.program_id(0)
    hg = jnp.zeros((ROWS, FF), F32)
    hu = jnp.zeros((ROWS, FF), F32)
    for r in range(N_REP):
        x = x_ref[0, :, r * SHARD : (r + 1) * SHARD]
        hg += dot_last(x, w_ref[0, r, :, 0:SHARD])
        hu += dot_last(x, w_ref[0, r, :, SHARD : 2 * SHARD])
    hg_ref[0] = hg
    hu_ref[0] = hu
    act = (hg * jax.nn.sigmoid(hg) * hu).astype(BF16)
    gate = gate_ref[0]
    start = pl.multiple_of(j * ROWS, 16)
    for r in range(N_REP):
        cols = slice(r * SHARD, (r + 1) * SHARD)
        eo = dot(act, w_ref[0, r, :, 2 * SHARD : 3 * SHARD]).astype(BF16)
        eo_ref[0, :, cols] = eo
        rows_ref[pl.ds(start, ROWS), cols] = (eo.astype(F32) * gate).astype(BF16)

    @pl.when(j == N_Y - 1)
    def _():
        for r in range(N_REP):
            cols = slice(r * SHARD, (r + 1) * SHARD)
            if r < PART:
                out_ref[:, cols] = dot(spread_ref[...], rows_ref[:, cols]).astype(BF16)
            else:
                to = slice((r - PART) * SHARD, (r - PART + 1) * SHARD)
                near_ref[:, to] = dot(spread_near_ref[...], rows_ref[:, cols]).astype(BF16)


def backward_kernel(
    c_ref, c_near_ref, p_ref, p_near_ref, x_ref, w_ref, gate_ref, slope_ref, eo_ref, hg_ref, hu_ref, router_ref, gain_ref, spread_ref,
    out_ref, router_grad_ref, gain_grad_ref, rows_ref,
):
    j = pl.program_id(0)
    gate = gate_ref[0]
    grad_act = jnp.zeros((ROWS, FF), F32)
    grad_gating = jnp.zeros((ROWS, 1), F32)
    for r in range(N_REP):
        cols = slice(r * SHARD, (r + 1) * SHARD)
        if r < PART:
            c = dot(p_ref[0], c_ref[:, cols])
        else:
            c = dot(p_near_ref[0], c_near_ref[:, (r - PART) * SHARD : (r - PART + 1) * SHARD])
        grad_gating += jnp.sum(c * eo_ref[0, :, cols].astype(F32), axis=1, keepdims=True)
        grad_act += dot_last((gate * c).astype(BF16), w_ref[0, r, :, 2 * SHARD : 3 * SHARD])
    grad_act = grad_act.astype(BF16).astype(F32)
    hg = hg_ref[0]
    s = jax.nn.sigmoid(hg)
    grad_hg = (grad_act * hu_ref[0] * s * (1.0 + hg * (1.0 - s))).astype(BF16)
    grad_hu = (grad_act * (hg * s)).astype(BF16)
    grad_logit = (grad_gating * slope_ref[0]).astype(BF16).astype(F32)
    start = pl.multiple_of(j * ROWS, 16)

    @pl.when(j == 0)
    def _():
        gain_grad_ref[...] = jnp.zeros_like(gain_grad_ref)

    for r in range(N_REP):
        cols = slice(r * SHARD, (r + 1) * SHARD)
        rows = dot(grad_hg, w_ref[0, r, :, 0:SHARD]) + dot(grad_hu, w_ref[0, r, :, SHARD : 2 * SHARD])
        rows = rows.astype(BF16).astype(F32) + grad_logit * router_ref[0, :, cols]
        x = x_ref[0, :, cols].astype(F32)
        router_grad_ref[0, :, cols] = jnp.sum(x * grad_logit, axis=0, keepdims=True)
        gain_grad_ref[:, cols] += jnp.sum(x * rows, axis=0, keepdims=True)
        rows_ref[pl.ds(start, ROWS), cols] = rows.astype(BF16)

    @pl.when(j == N_Y - 1)
    def _():
        gain_grad_ref[...] = gain_grad_ref[...] / gain_ref[...]
        for r in range(N_REP):
            cols = slice(r * SHARD, (r + 1) * SHARD)
            out_ref[:, cols] = dot(spread_ref[...], rows_ref[:, cols]).astype(BF16)


def whole(*shape):
    return pl.BlockSpec(shape, lambda j: (0,) * len(shape), pipeline_mode=pl.Buffered(1))


def each(*shape):
    return pl.BlockSpec((1,) + shape, lambda j: (j,) + (0,) * len(shape))


PARAMS = pltpu.CompilerParams(dimension_semantics=("arbitrary",), vmem_limit_bytes=42 * 1024 * 1024)


def expert_forward(x, weights, gate, spread, spread_near):
    shape = jax.ShapeDtypeStruct
    return pl.pallas_call(
        forward_kernel,
        grid=(N_Y,),
        in_specs=[each(ROWS, D), each(N_REP, FF, 3 * SHARD), each(ROWS, 1)]
        + [whole(COLUMN, N_Y * ROWS)] * 2,
        out_specs=[each(ROWS, D), each(ROWS, FF), each(ROWS, FF)]
        + [whole(COLUMN, PART * SHARD), whole(COLUMN, D - PART * SHARD)],
        out_shape=[
            shape((N_Y, ROWS, D), BF16),
            shape((N_Y, ROWS, FF), F32),
            shape((N_Y, ROWS, FF), F32),
            shape((COLUMN, PART * SHARD), BF16),
            shape((COLUMN, D - PART * SHARD), BF16),
        ],
        scratch_shapes=[pltpu.VMEM((N_Y * ROWS, D), BF16)],
        compiler_params=PARAMS,
        name="expert_forward",
    )(x, weights, gate, spread, spread_near)


def expert_backward(c, c_near, pick, pick_near, x, weights, gate, slope, eo, hg, hu, router, gain, spread):
    shape = jax.ShapeDtypeStruct
    return pl.pallas_call(
        backward_kernel,
        grid=(N_Y,),
        in_specs=[
            whole(COLUMN, PART * SHARD), whole(COLUMN, D - PART * SHARD), each(ROWS, COLUMN), each(ROWS, COLUMN),
            each(ROWS, D), each(N_REP, FF, 3 * SHARD), each(ROWS, 1), each(ROWS, 1),
            each(ROWS, D), each(ROWS, FF), each(ROWS, FF), each(1, D), whole(1, D), whole(COLUMN, N_Y * ROWS),
        ],
        out_specs=[whole(COLUMN, D), each(1, D), whole(1, D)],
        out_shape=[shape((COLUMN, D), BF16), shape((N_Y, 1, D), F32), shape((1, D), F32)],
        scratch_shapes=[pltpu.VMEM((N_Y * ROWS, D), BF16)],
        compiler_params=PARAMS,
        name="expert_backward",
    )(c, c_near, pick, pick_near, x, weights, gate, slope, eo, hg, hu, router, gain, spread)


def ring_gather(block, chains):
    width = block.shape[1] // chains
    parts = []
    for i in range(chains):
        up = [block[:, i * width : (i + 1) * width]]
        down = [up[0]]
        parts.append((up, down))
    for step in range(4):
        for up, down in parts:
            up.append(lax.ppermute(up[-1], "z", UP))
            if step < 3:
                down.append(lax.ppermute(down[-1], "z", DOWN))
    return [parts[i][0] + parts[i][1][:0:-1] for i in range(chains)]


def in_order(blocks, z):
    stacked = jnp.stack([jnp.concatenate(b, axis=1) for b in zip(*blocks)])
    backwards = jnp.stack([stacked[(-k) % N_Z] for k in range(N_Z)])
    return jnp.roll(backwards, z, axis=0)


def shards(latent, targets, norm_gain, router, expert_ids, gate_valid, w_gate, w_up, w_down):
    y_axes = ("y", "x", "c")
    z = lax.axis_index("z")
    own = jnp.concatenate([w_gate[0].T, w_up[0].T, w_down[0]], axis=1)
    weights = lax.all_gather(own, y_axes, axis=0, tiled=False).reshape(N_Y, N_REP, FF, 3 * SHARD)

    inv_scale = lax.rsqrt(jnp.mean(latent * latent, axis=-1, keepdims=True) + EPS)
    normed = (latent * inv_scale * norm_gain).astype(BF16)
    codes = (expert_ids[0] + 32 * gate_valid[0]).T
    codes = jnp.concatenate([codes, jnp.zeros((2, LOCAL), jnp.int32)], axis=0)

    column = jnp.concatenate([jnp.concatenate(b, axis=1) for b in zip(*ring_gather(normed, 2))], axis=0)
    column_codes = jnp.concatenate(ring_gather(codes, 1)[0], axis=1)[:TOP]
    ids, valid = column_codes % 32, column_codes // 32

    mine = jnp.arange(N_Y, dtype=jnp.int32) * N_Z + z
    hit = ids[None] == mine[:, None, None]
    chosen = jnp.any(hit, axis=1)
    valid_here = jnp.sum(jnp.where(hit, valid[None], 0), axis=1).astype(F32)
    token = jnp.arange(COLUMN, dtype=jnp.int32)
    earlier = (token[:, None] < token[None, :]).astype(BF16)
    rank = dot(chosen.astype(BF16), earlier).astype(jnp.int32)
    rank = jnp.where(chosen, rank, -1)
    slot = jnp.arange(ROWS, dtype=jnp.int32)
    at = rank[:, None, :] == slot[None, :, None]
    pick_near = at.astype(BF16)
    spread_near = spread_of(rank, slot)
    x = dot(pick_near.reshape(N_Y * ROWS, COLUMN), column).astype(BF16).reshape(N_Y, ROWS, D)
    rank = by_owner(rank, z)
    pick = (rank[:, None, :] == slot[None, :, None]).astype(BF16)
    spread = spread_of(rank, slot)
    router_here = lax.dynamic_index_in_dim(router.reshape(D, N_Y, N_Z), z, 2, keepdims=False).T.astype(F32)
    logit = jnp.sum(x.astype(F32) * router_here[:, None, :], axis=2)
    sigmoid_pick = jax.nn.sigmoid(logit)
    valid_row = jnp.sum(jnp.where(at, valid_here[:, None, :], 0.0), axis=2)
    gate = (sigmoid_pick * valid_row)[:, :, None]
    slope = (valid_row * sigmoid_pick * (1.0 - sigmoid_pick))[:, :, None]

    eo, hg, hu, mixed, mixed_near = expert_forward(x, weights, gate, spread, spread_near)
    base = latent - targets[0].astype(F32)
    cut = PART * SHARD
    first, second = lax.optimization_barrier((scatter_sum(mixed), ring_sum(mixed_near)))
    first = base[:, :cut] + first.astype(F32)
    second = base[:, cut:] + second
    c = gather_column(first.astype(BF16))
    c_near = jnp.concatenate(ring_gather(second.astype(BF16), 1)[0], axis=0)
    cotangent = jnp.concatenate([first, second], axis=1)
    back, router_grad, gain_grad = expert_backward(
        c, c_near, pick, pick_near, x, weights, gate, slope, eo, hg, hu, router_here[:, None, :], norm_gain[None], spread
    )
    grad_normed = scatter_sum(back).astype(F32)

    sums = jnp.concatenate([router_grad[:, 0], gain_grad, jnp.zeros((3, D), F32)], axis=0)
    sums = sums + lax.ppermute(sums, "c", [(0, 1), (1, 0)])
    for axis in ("x", "y"):
        for flip in (1, 2):
            sums = sums + lax.ppermute(sums, axis, [(i, i ^ flip) for i in range(4)])
    sums = in_order(ring_gather(sums, 1), z)
    grad_router = sums[:, :N_Y].transpose(2, 1, 0).reshape(D, N_Y * N_Z)
    grad_gain = jnp.sum(sums[:, N_Y], axis=0)

    scaled = grad_normed * norm_gain
    cube = inv_scale * inv_scale * inv_scale
    grad_latent = (
        cotangent + inv_scale * scaled - latent * cube * jnp.mean(scaled * latent, axis=-1, keepdims=True)
    )
    return grad_latent, grad_router, grad_gain


def by_owner(values, z):
    blocks = values.reshape(-1, N_Z, LOCAL)
    return jnp.stack([lax.dynamic_index_in_dim(blocks, (z - k) % N_Z, 1, keepdims=False) for k in range(N_Z)], axis=1).reshape(
        -1, COLUMN
    )


def spread_of(rank, slot):
    return (rank.T[:, :, None] == slot[None, None, :]).astype(BF16).reshape(COLUMN, N_Y * ROWS)


def ring_sum(partial):
    blocks = [partial[k * LOCAL : (k + 1) * LOCAL] for k in range(N_Z)]
    up, down = blocks[4], blocks[3]
    for k in (5, 6, 7):
        up = lax.ppermute(up, "z", UP)
        up = (up.astype(F32) + blocks[k].astype(F32)).astype(BF16)
        if k < 7:
            down = lax.ppermute(down, "z", DOWN)
            down = (down.astype(F32) + blocks[7 - k].astype(F32)).astype(BF16)
    up = lax.ppermute(up, "z", UP)
    down = lax.ppermute(down, "z", DOWN)
    return blocks[0].astype(F32) + up.astype(F32) + down.astype(F32)


def scatter_sum(partial):
    return lax.psum_scatter(partial, "z", scatter_dimension=0, tiled=True)


def gather_column(block):
    return lax.all_gather(block, "z", axis=0, tiled=True)


def solution(mesh):
    split = Mesh(mesh.devices.reshape(N_X, N_C, N_Y, N_Z), ("x", "c", "y", "z"))
    every = ("x", "c", "y", "z")
    rep, exp = ("x", "c"), ("y", "z")
    return jax.shard_map(
        shards,
        mesh=split,
        in_specs=(
            P(every, None),
            P(None, every, None),
            P(),
            P(),
            P(None, every, None),
            P(None, every, None),
            P(exp, rep, None),
            P(exp, rep, None),
            P(exp, None, rep),
        ),
        out_specs=(P(every, None), P(), P()),
        check_vma=False,
    )
```

```python
import jax
import jax.numpy as jnp
from jax import lax
from jax.experimental import pallas as pl
from jax.experimental.pallas import tpu as pltpu
from jax.sharding import Mesh, PartitionSpec as P

N_X, N_C, N_Y, N_Z = 4, 2, 4, 8
TOP = 6
LOCAL = 128
COLUMN = N_Z * LOCAL
CAP = 25
ROWS = 208
D = 2048
FF = 704
N_REP = N_X * N_C
SHARD = D // N_REP
PART = 5
EPS = 1e-06
F32, BF16 = jnp.float32, jnp.bfloat16
UP = [(i, (i + 1) % N_Z) for i in range(N_Z)]
DOWN = [(i, (i - 1) % N_Z) for i in range(N_Z)]


def dot(left, right):
    return jnp.dot(left, right, preferred_element_type=F32)


def dot_last(left, right):
    return lax.dot_general(left, right, (((1,), (1,)), ((), ())), preferred_element_type=F32)


def forward_kernel(
    x_ref, w_ref, gate_ref, spread_ref, spread_near_ref, eo_ref, hg_ref, hu_ref, out_ref, near_ref, rows_ref
):
    j = pl.program_id(0)
    hg = jnp.zeros((ROWS, FF), F32)
    hu = jnp.zeros((ROWS, FF), F32)
    for r in range(N_REP):
        x = x_ref[0, :, r * SHARD : (r + 1) * SHARD]
        hg += dot_last(x, w_ref[0, r, :, 0:SHARD])
        hu += dot_last(x, w_ref[0, r, :, SHARD : 2 * SHARD])
    hg_ref[0] = hg
    hu_ref[0] = hu
    act = (hg * jax.nn.sigmoid(hg) * hu).astype(BF16)
    gate = gate_ref[0]
    start = pl.multiple_of(j * ROWS, 16)
    for r in range(N_REP):
        cols = slice(r * SHARD, (r + 1) * SHARD)
        eo = dot(act, w_ref[0, r, :, 2 * SHARD : 3 * SHARD]).astype(BF16)
        eo_ref[0, :, cols] = eo
        rows_ref[pl.ds(start, ROWS), cols] = (eo.astype(F32) * gate).astype(BF16)

    @pl.when(j == N_Y - 1)
    def _():
        for r in range(N_REP):
            cols = slice(r * SHARD, (r + 1) * SHARD)
            if r < PART:
                out_ref[:, cols] = dot(spread_ref[...], rows_ref[:, cols]).astype(BF16)
            else:
                to = slice((r - PART) * SHARD, (r - PART + 1) * SHARD)
                near_ref[:, to] = dot(spread_near_ref[...], rows_ref[:, cols]).astype(BF16)


def backward_kernel(
    c_ref, c_near_ref, p_ref, p_near_ref, x_ref, w_ref, gate_ref, slope_ref, eo_ref, hg_ref, hu_ref, router_ref, gain_ref, spread_ref,
    out_ref, router_grad_ref, gain_grad_ref, rows_ref,
):
    j = pl.program_id(0)
    gate = gate_ref[0]
    grad_act = jnp.zeros((ROWS, FF), F32)
    grad_gating = jnp.zeros((ROWS, 1), F32)
    for r in range(N_REP):
        cols = slice(r * SHARD, (r + 1) * SHARD)
        if r < PART:
            c = dot(p_ref[0], c_ref[:, cols])
        else:
            c = dot(p_near_ref[0], c_near_ref[:, (r - PART) * SHARD : (r - PART + 1) * SHARD])
        grad_gating += jnp.sum(c * eo_ref[0, :, cols].astype(F32), axis=1, keepdims=True)
        grad_act += dot_last((gate * c).astype(BF16), w_ref[0, r, :, 2 * SHARD : 3 * SHARD])
    grad_act = grad_act.astype(BF16).astype(F32)
    hg = hg_ref[0]
    s = jax.nn.sigmoid(hg)
    grad_hg = (grad_act * hu_ref[0] * s * (1.0 + hg * (1.0 - s))).astype(BF16)
    grad_hu = (grad_act * (hg * s)).astype(BF16)
    grad_logit = (grad_gating * slope_ref[0]).astype(BF16).astype(F32)
    start = pl.multiple_of(j * ROWS, 16)

    @pl.when(j == 0)
    def _():
        gain_grad_ref[...] = jnp.zeros_like(gain_grad_ref)

    for r in range(N_REP):
        cols = slice(r * SHARD, (r + 1) * SHARD)
        rows = dot(grad_hg, w_ref[0, r, :, 0:SHARD]) + dot(grad_hu, w_ref[0, r, :, SHARD : 2 * SHARD])
        rows = rows.astype(BF16).astype(F32) + grad_logit * router_ref[0, :, cols]
        x = x_ref[0, :, cols].astype(F32)
        router_grad_ref[0, :, cols] = jnp.sum(x * grad_logit, axis=0, keepdims=True)
        gain_grad_ref[:, cols] += jnp.sum(x * rows, axis=0, keepdims=True)
        rows_ref[pl.ds(start, ROWS), cols] = rows.astype(BF16)

    @pl.when(j == N_Y - 1)
    def _():
        gain_grad_ref[...] = gain_grad_ref[...] / gain_ref[...]
        for r in range(N_REP):
            cols = slice(r * SHARD, (r + 1) * SHARD)
            out_ref[:, cols] = dot(spread_ref[...], rows_ref[:, cols]).astype(BF16)


def whole(*shape):
    return pl.BlockSpec(shape, lambda j: (0,) * len(shape))


def each(*shape):
    return pl.BlockSpec((1,) + shape, lambda j: (j,) + (0,) * len(shape))


PARAMS = pltpu.CompilerParams(dimension_semantics=("arbitrary",), vmem_limit_bytes=60 * 1024 * 1024)


def expert_forward(x, weights, gate, spread, spread_near):
    shape = jax.ShapeDtypeStruct
    return pl.pallas_call(
        forward_kernel,
        grid=(N_Y,),
        in_specs=[each(ROWS, D), each(N_REP, FF, 3 * SHARD), each(ROWS, 1)]
        + [whole(COLUMN, N_Y * ROWS)] * 2,
        out_specs=[each(ROWS, D), each(ROWS, FF), each(ROWS, FF)]
        + [whole(COLUMN, PART * SHARD), whole(COLUMN, D - PART * SHARD)],
        out_shape=[
            shape((N_Y, ROWS, D), BF16),
            shape((N_Y, ROWS, FF), F32),
            shape((N_Y, ROWS, FF), F32),
            shape((COLUMN, PART * SHARD), BF16),
            shape((COLUMN, D - PART * SHARD), BF16),
        ],
        scratch_shapes=[pltpu.VMEM((N_Y * ROWS, D), BF16)],
        compiler_params=PARAMS,
        name="expert_forward",
    )(x, weights, gate, spread, spread_near)


def expert_backward(c, c_near, pick, pick_near, x, weights, gate, slope, eo, hg, hu, router, gain, spread):
    shape = jax.ShapeDtypeStruct
    return pl.pallas_call(
        backward_kernel,
        grid=(N_Y,),
        in_specs=[
            whole(COLUMN, PART * SHARD), whole(COLUMN, D - PART * SHARD), each(ROWS, COLUMN), each(ROWS, COLUMN),
            each(ROWS, D), each(N_REP, FF, 3 * SHARD), each(ROWS, 1), each(ROWS, 1),
            each(ROWS, D), each(ROWS, FF), each(ROWS, FF), each(1, D), whole(1, D), whole(COLUMN, N_Y * ROWS),
        ],
        out_specs=[whole(COLUMN, D), each(1, D), whole(1, D)],
        out_shape=[shape((COLUMN, D), BF16), shape((N_Y, 1, D), F32), shape((1, D), F32)],
        scratch_shapes=[pltpu.VMEM((N_Y * ROWS, D), BF16)],
        compiler_params=PARAMS,
        name="expert_backward",
    )(c, c_near, pick, pick_near, x, weights, gate, slope, eo, hg, hu, router, gain, spread)


def ring_gather(block, chains):
    width = block.shape[1] // chains
    parts = []
    for i in range(chains):
        up = [block[:, i * width : (i + 1) * width]]
        down = [up[0]]
        parts.append((up, down))
    for step in range(4):
        for up, down in parts:
            up.append(lax.ppermute(up[-1], "z", UP))
            if step < 3:
                down.append(lax.ppermute(down[-1], "z", DOWN))
    return [parts[i][0] + parts[i][1][:0:-1] for i in range(chains)]


def in_order(blocks, z):
    stacked = jnp.stack([jnp.concatenate(b, axis=1) for b in zip(*blocks)])
    backwards = jnp.stack([stacked[(-k) % N_Z] for k in range(N_Z)])
    return jnp.roll(backwards, z, axis=0)


def shards(latent, targets, norm_gain, router, expert_ids, gate_valid, w_gate, w_up, w_down):
    y_axes = ("y", "x", "c")
    z = lax.axis_index("z")
    own = jnp.concatenate([w_gate[0].T, w_up[0].T, w_down[0]], axis=1)
    weights = lax.all_gather(own, y_axes, axis=0, tiled=False).reshape(N_Y, N_REP, FF, 3 * SHARD)

    inv_scale = lax.rsqrt(jnp.mean(latent * latent, axis=-1, keepdims=True) + EPS)
    normed = (latent * inv_scale * norm_gain).astype(BF16)
    codes = (expert_ids[0] + 32 * gate_valid[0]).T
    codes = jnp.concatenate([codes, jnp.zeros((2, LOCAL), jnp.int32)], axis=0)

    column = jnp.concatenate([jnp.concatenate(b, axis=1) for b in zip(*ring_gather(normed, 2))], axis=0)
    column_codes = jnp.concatenate(ring_gather(codes, 1)[0], axis=1)[:TOP]
    ids, valid = column_codes % 32, column_codes // 32

    mine = jnp.arange(N_Y, dtype=jnp.int32) * N_Z + z
    hit = ids[None] == mine[:, None, None]
    chosen = jnp.any(hit, axis=1)
    valid_here = jnp.sum(jnp.where(hit, valid[None], 0), axis=1).astype(F32)
    token = jnp.arange(COLUMN, dtype=jnp.int32)
    earlier = (token[:, None] < token[None, :]).astype(BF16)
    rank = dot(chosen.astype(BF16), earlier).astype(jnp.int32)
    rank = jnp.where(chosen, rank, -1)
    slot = jnp.arange(ROWS, dtype=jnp.int32)
    at = rank[:, None, :] == slot[None, :, None]
    pick_near = at.astype(BF16)
    spread_near = spread_of(rank, slot)
    x = dot(pick_near.reshape(N_Y * ROWS, COLUMN), column).astype(BF16).reshape(N_Y, ROWS, D)
    rank = by_owner(rank, z)
    pick = (rank[:, None, :] == slot[None, :, None]).astype(BF16)
    spread = spread_of(rank, slot)
    router_here = lax.dynamic_index_in_dim(router.reshape(D, N_Y, N_Z), z, 2, keepdims=False).T.astype(F32)
    logit = jnp.sum(x.astype(F32) * router_here[:, None, :], axis=2)
    sigmoid_pick = jax.nn.sigmoid(logit)
    valid_row = jnp.sum(jnp.where(at, valid_here[:, None, :], 0.0), axis=2)
    gate = (sigmoid_pick * valid_row)[:, :, None]
    slope = (valid_row * sigmoid_pick * (1.0 - sigmoid_pick))[:, :, None]

    eo, hg, hu, mixed, mixed_near = expert_forward(x, weights, gate, spread, spread_near)
    base = latent - targets[0].astype(F32)
    cut = PART * SHARD
    first, second = lax.optimization_barrier((scatter_sum(mixed), ring_sum(mixed_near)))
    first = base[:, :cut] + first.astype(F32)
    second = base[:, cut:] + second
    c = gather_column(first.astype(BF16))
    c_near = jnp.concatenate(ring_gather(second.astype(BF16), 1)[0], axis=0)
    cotangent = jnp.concatenate([first, second], axis=1)
    back, router_grad, gain_grad = expert_backward(
        c, c_near, pick, pick_near, x, weights, gate, slope, eo, hg, hu, router_here[:, None, :], norm_gain[None], spread
    )
    grad_normed = scatter_sum(back).astype(F32)

    sums = jnp.concatenate([router_grad[:, 0], gain_grad, jnp.zeros((3, D), F32)], axis=0)
    sums = sums + lax.ppermute(sums, "c", [(0, 1), (1, 0)])
    for axis in ("x", "y"):
        for flip in (1, 2):
            sums = sums + lax.ppermute(sums, axis, [(i, i ^ flip) for i in range(4)])
    straight = [lax.ppermute(sums, "z", [(i, (i + k) % N_Z) for i in range(N_Z)]) for k in range(1, N_Z)]
    sums = in_order([[sums] + straight], z)
    grad_router = sums[:, :N_Y].transpose(2, 1, 0).reshape(D, N_Y * N_Z)
    grad_gain = jnp.sum(sums[:, N_Y], axis=0)

    scaled = grad_normed * norm_gain
    cube = inv_scale * inv_scale * inv_scale
    grad_latent = (
        cotangent + inv_scale * scaled - latent * cube * jnp.mean(scaled * latent, axis=-1, keepdims=True)
    )
    return grad_latent, grad_router, grad_gain


def by_owner(values, z):
    blocks = values.reshape(-1, N_Z, LOCAL)
    return jnp.stack([lax.dynamic_index_in_dim(blocks, (z - k) % N_Z, 1, keepdims=False) for k in range(N_Z)], axis=1).reshape(
        -1, COLUMN
    )


def spread_of(rank, slot):
    return (rank.T[:, :, None] == slot[None, None, :]).astype(BF16).reshape(COLUMN, N_Y * ROWS)


def ring_sum(partial):
    blocks = [partial[k * LOCAL : (k + 1) * LOCAL] for k in range(N_Z)]
    up, down = blocks[4], blocks[3]
    for k in (5, 6, 7):
        up = lax.ppermute(up, "z", UP)
        up = (up.astype(F32) + blocks[k].astype(F32)).astype(BF16)
        if k < 7:
            down = lax.ppermute(down, "z", DOWN)
            down = (down.astype(F32) + blocks[7 - k].astype(F32)).astype(BF16)
    up = lax.ppermute(up, "z", UP)
    down = lax.ppermute(down, "z", DOWN)
    return blocks[0].astype(F32) + up.astype(F32) + down.astype(F32)


def scatter_sum(partial):
    return lax.psum_scatter(partial, "z", scatter_dimension=0, tiled=True)


def gather_column(block):
    return lax.all_gather(block, "z", axis=0, tiled=True)


def solution(mesh):
    split = Mesh(mesh.devices.reshape(N_X, N_C, N_Y, N_Z), ("x", "c", "y", "z"))
    every = ("x", "c", "y", "z")
    rep, exp = ("x", "c"), ("y", "z")
    return jax.shard_map(
        shards,
        mesh=split,
        in_specs=(
            P(every, None),
            P(None, every, None),
            P(),
            P(),
            P(None, every, None),
            P(None, every, None),
            P(exp, rep, None),
            P(exp, rep, None),
            P(exp, None, rep),
        ),
        out_specs=(P(every, None), P(), P()),
        check_vma=False,
    )
```
